512 devices in a mesh: lat: 16 (over y, x), lon: 32 (over z, core).
Axes of the slice: x: 4, y: 4, z: 16, core: 2. Of those that a mesh axis runs over, the one named last changes fastest.
Arguments:
- grad_field: bfloat16 [720, 1440, 128], P('lat', 'lon'), may hold values from -6 to 6
- legendre: bfloat16 [384, 720, 672], P('lon', 'lat'), may hold values from -0.21875 to 0.21875
Outputs:
- grad_coeff: bfloat16 [672, 384, 2, 128], P(None, 'lon')
The draws below stay inside these ranges and needn't reach their ends.
All inputs are finite; a program needn't handle non-finite values.
Results may differ from the reference program's by a relative error of at most 0.023.
Values may be sent and summed in bfloat16 or wider, within the bound.
No kernel may reach another device: no remote copies, remote signals or barrier semaphores. Data moves between devices by JAX's collectives and lax.ppermute only.
A program may use at most 64 MiB of HBM per device.

```python
import jax
import jax.numpy as jnp
from jax import lax

DEGREES = 672
ORDERS = 384
NLON = 1440
NLAT = 720
CH = 128
LAT_DEV = 45
N_LAT = 16


def block_levels(key, extent, pieces, low, top_value):
    level, own = 1.0, jax.random.fold_in(key, 6)
    for axis_at, blocks in pieces:
        draws = jnp.exp(jax.random.uniform(jax.random.fold_in(own, axis_at), (blocks,), jnp.float32, low / len(pieces), top_value / len(pieces)))
        level = level * jnp.repeat(draws, extent[axis_at] // blocks).reshape([-1 if axis == axis_at else 1 for axis in range(len(extent))])
    return level


def bell_draw(stream_key, dims, width, limit, pieces=(), kind=jnp.bfloat16):
    level = block_levels(stream_key, dims, pieces, -0.22, 0.18) if pieces else 1.0
    drawn = jax.random.normal(stream_key, dims, jnp.float32) * width * level
    return jnp.minimum(jnp.maximum(drawn, -limit), limit).astype(kind)


def setup_inputs(seed: int = 0) -> dict:
    streams_of = jax.random.split(jax.random.key(seed), 3)
    return {
        "grad_field": bell_draw(streams_of[0], (NLAT, NLON, CH), 1.0, 6.0, ((0, 16), (1, 32))),
        "legendre": bell_draw(streams_of[1], (ORDERS, NLAT, DEGREES), NLAT ** -0.5, 0.21875, ((0, 32), (1, 16))),
    }


def fourier_table(first_column, columns):
    column_ids = first_column + jnp.arange(columns, dtype=jnp.int32)
    order_ids = jnp.arange(ORDERS, dtype=jnp.int32)
    phases = (column_ids[:, None] * order_ids[None, :] % NLON).astype(jnp.float32) * (2.0 * jnp.pi / NLON)
    order_weight = jnp.where(order_ids == 0, 1.0, 2.0).astype(jnp.float32) / jnp.sqrt(jnp.float32(NLON))
    cosines = order_weight[None, :] * jnp.cos(phases)
    sines = -order_weight[None, :] * jnp.sin(phases)
    return jnp.stack([cosines, sines]).astype(jnp.bfloat16)

def reference(grad_field, legendre):
    table = fourier_table(0, NLON)
    spectrum = jnp.einsum('kjc,rjm->mkrc', grad_field.astype(jnp.float32), table.astype(jnp.float32)).astype(jnp.bfloat16)
    degree_ids = jnp.arange(DEGREES, dtype=jnp.int32)
    order_ids = jnp.arange(ORDERS, dtype=jnp.int32)
    allowed = degree_ids[None, None, :] >= order_ids[:, None, None]
    masked = jnp.where(allowed, legendre, jnp.zeros_like(legendre))
    running_sum = jnp.zeros((DEGREES, ORDERS, 2, CH), jnp.float32)
    for block in range(N_LAT):
        lat_legendre = masked[:, block * LAT_DEV:(block + 1) * LAT_DEV].astype(jnp.float32)
        lat_spectrum = spectrum[:, block * LAT_DEV:(block + 1) * LAT_DEV].astype(jnp.float32)
        block_part = jnp.einsum('mkl,mkrc->lmrc', lat_legendre, lat_spectrum).astype(jnp.bfloat16)
        block_part = lax.optimization_barrier(block_part)
        running_sum = running_sum + block_part.astype(jnp.float32)
    return running_sum.astype(jnp.bfloat16)
```

```python
import jax
import jax.numpy as jnp
from jax import lax
from jax.experimental import pallas as pl
from jax.experimental.pallas import tpu as pltpu
from jax.sharding import Mesh, PartitionSpec as P

DEGREES = 672
ORDERS = 384
NLON = 1440
CH = 128
SIDE = 4
LAT = SIDE * SIDE
LON = 32
ROWS = 45
COLS = 45
PAD = 48
HELD = ORDERS // LON
OWN = HELD // SIDE
EXTRA = ROWS - LON
SENT = PAD + PAD // 2
BACK = 40
F32, BF16 = jnp.float32, jnp.bfloat16
VMEM_LIMIT = 48 * 1024 * 1024


def call(body, out_shape, scratch=(), n_in=1):
    whole = pl.BlockSpec(memory_space=pltpu.VMEM)
    return pl.pallas_call(
        body,
        out_shape=out_shape,
        in_specs=[whole] * n_in,
        out_specs=whole,
        scratch_shapes=list(scratch),
        compiler_params=pltpu.CompilerParams(vmem_limit_bytes=VMEM_LIMIT),
    )


def left_half(shape):
    return lax.broadcasted_iota(jnp.int32, shape, len(shape) - 1) < CH // 2


def pack_rows(grad_ref, out_ref, rows):
    rows[...] = jnp.zeros_like(rows)
    half = PAD // 2
    left = left_half((half, CH))
    for d in range(LON):
        rows[0:COLS, :] = grad_ref[d].astype(F32)
        out_ref[d, 0:PAD, :] = rows[...].astype(BF16)
    for extra in range(EXTRA):
        rows[0:COLS, :] = grad_ref[LON + extra].astype(F32)
        early, late = rows[0:half, :], rows[half:PAD, :]
        first = jnp.where(left, early, pltpu.roll(late, CH // 2, 1))
        second = jnp.where(left, pltpu.roll(early, CH // 2, 1), late)
        out_ref[2 * extra, PAD:SENT, :] = first.astype(BF16)
        out_ref[2 * extra + 1, PAD:SENT, :] = second.astype(BF16)
    for d in range(2 * EXTRA, LON):
        out_ref[d, PAD:SENT, :] = jnp.zeros((half, CH), BF16)


def spectrum_rows(x_ref, table_ref, out_ref, both):
    half = PAD // 2
    left = left_half((half, CH))
    for d in range(LON):
        at = d * PAD
        both[at : at + PAD, 0:CH] = x_ref[d, 0:PAD, :]
        packed = x_ref[d, PAD:SENT, :].astype(F32)
        early = jnp.where(left, packed, 0.0)
        late = jnp.where(left, pltpu.roll(packed, CH // 2, 1), 0.0)
        both[at : at + PAD, CH : 2 * CH] = jnp.concatenate([early, late], 0).astype(BF16)
    n = 2 * HELD
    found = jnp.dot(table_ref[...], both[...], preferred_element_type=F32)
    left8 = left_half((8, CH))
    for d in range(LON):
        whole = found[d * n : (d + 1) * n, 0:CH]
        part = found[d * n : (d + 1) * n, CH : 2 * CH]
        mixed = jnp.where(left8, part[0:8], pltpu.roll(part[16:24], CH // 2, 1))
        out_ref[d] = jnp.concatenate([whole, mixed, part[8:16]], 0).astype(BF16)


def turn_rows(r_ref, out_ref, flat):
    for d in range(LON):
        flat[d * BACK : (d + 1) * BACK, :] = r_ref[d].astype(F32)
    n = 2 * HELD
    left = left_half((16, CH))
    for order in range(HELD):
        colour, place = divmod(order, OWN)
        for part in range(2):
            i = part * HELD + order
            lanes = slice(part * CH, (part + 1) * CH)
            main = flat[pl.ds(i, LON, stride=BACK), :]
            at = n + (i if i < 16 else i - 16)
            even = flat[pl.ds(at, 16, stride=2 * BACK), :]
            odd = flat[pl.ds(BACK + at, 16, stride=2 * BACK), :]
            if i < 16:
                rest = jnp.where(left, even, pltpu.roll(odd, CH // 2, 1))
            else:
                rest = jnp.where(left, pltpu.roll(even, CH // 2, 1), odd)
            column = jnp.concatenate([main, rest], 0).astype(BF16)
            for t in range(LAT):
                if (t % SIDE + 2 * (t // SIDE)) % SIDE == colour:
                    out_ref[t, place, :, lanes] = column


def turn_legendre(p0_ref, p1_ref, p2_ref, p3_ref, out_ref, tall):
    for place in range(OWN):
        for hop, ref in enumerate((p0_ref, p1_ref, p2_ref, p3_ref)):
            for shift in range(SIDE):
                at = (hop * SIDE + shift) * PAD
                tall[at : at + PAD, :] = ref[shift, place].astype(F32)
        out_ref[place] = tall[...].T[0:DEGREES].astype(BF16)


def legendre_sum(s_ref, p_ref, out_ref, gathered, spread):
    y, x = lax.axis_index("y"), lax.axis_index("x")
    for hop in range(SIDE):
        for shift in range(SIDE):
            row = lax.rem(y + (SIDE - hop), SIDE)
            column = lax.rem(x + (3 * SIDE - 2 * hop - shift), SIDE)
            at = (hop * SIDE + shift) * PAD
            for place in range(OWN):
                gathered[place, at : at + PAD, :] = s_ref[row * SIDE + column, place]
    for place in range(OWN):
        found = jnp.dot(p_ref[place], gathered[place], preferred_element_type=F32)
        for part in range(2):
            rows = pl.ds(2 * place + part, DEGREES, stride=2 * OWN)
            spread[rows, :] = found[:, part * CH : (part + 1) * CH]
    out_ref[...] = spread[...].astype(BF16)


def fourier_table():
    rows = jnp.arange(2 * ORDERS, dtype=jnp.int32)[:, None]
    columns = jnp.arange(LON * PAD, dtype=jnp.int32)[None, :]
    part = rows % (2 * HELD) // HELD
    order = rows // (2 * HELD) * HELD + rows % HELD
    within = columns % PAD
    longitude = columns // PAD * COLS + within
    phases = ((longitude * order + part * (NLON // 4)) % NLON).astype(F32)
    weight = jnp.where(order == 0, 1.0, 2.0).astype(F32) / jnp.sqrt(F32(NLON))
    values = weight * jnp.cos(phases * (2.0 * jnp.pi / NLON))
    return jnp.where(within < COLS, values, 0.0).astype(BF16)


def along(axis, value, step):
    return lax.ppermute(value, axis, [(i, (i + step) % SIDE) for i in range(SIDE)])


def same_colour(value, step):
    pairs = []
    for y in range(SIDE):
        for x in range(SIDE):
            to = (y + step) % SIDE * SIDE + (x + 2 * step) % SIDE
            pairs.append((y * SIDE + x, to))
    return lax.ppermute(value, ("y", "x"), pairs)


def on_device(grad_field, legendre):
    y, x, lon = lax.axis_index("y"), lax.axis_index("x"), lax.axis_index("lon")
    colour = (x + 2 * y) % SIDE
    struct = jax.ShapeDtypeStruct

    packed = call(
        pack_rows, struct((LON, SENT, CH), BF16), [pltpu.VMEM((PAD, CH), F32)]
    )(grad_field)
    row_columns = lax.all_to_all(packed, "lon", 0, 0, tiled=True)

    order_ids = lon * HELD + jnp.arange(HELD, dtype=jnp.int32)
    degree_ids = jnp.arange(DEGREES, dtype=jnp.int32)
    allowed = degree_ids[None, None, :] >= order_ids[:, None, None]
    masked = jnp.where(allowed, legendre, jnp.zeros_like(legendre))
    masked = jnp.pad(masked, ((0, 0), (0, PAD - ROWS), (0, 768 - DEGREES)))
    masked = masked.reshape(SIDE, OWN, PAD, 768)
    line = [lax.dynamic_index_in_dim(masked, colour, 0, keepdims=False)]
    for step in (1, 2, 3):
        theirs = lax.dynamic_index_in_dim(masked, (colour + step) % SIDE, 0, keepdims=False)
        line.append(along("x", theirs, step))
    line = jnp.stack(line)
    lines = [line] + [same_colour(line, step) for step in (1, 2, 3)]

    returned = call(
        spectrum_rows,
        struct((LON, BACK, CH), BF16),
        [pltpu.VMEM((LON * PAD, 2 * CH), BF16)],
        n_in=2,
    )(row_columns, fourier_table())
    by_sender = lax.all_to_all(returned, "lon", 0, 0, tiled=True)
    turned = call(
        turn_rows,
        struct((LAT, OWN, PAD, 2 * CH), BF16),
        [pltpu.VMEM((LON * BACK, CH), F32)],
    )(by_sender)
    spectrum = lax.all_to_all(turned, ("y", "x"), 0, 0, tiled=True)

    upright = call(
        turn_legendre,
        struct((OWN, DEGREES, LAT * PAD), BF16),
        [pltpu.VMEM((LAT * PAD, 768), F32)],
        n_in=4,
    )(*lines)
    own = call(
        legendre_sum,
        struct((DEGREES * OWN * 2, CH), BF16),
        [
            pltpu.VMEM((OWN, LAT * PAD, 2 * CH), BF16),
            pltpu.VMEM((DEGREES * OWN * 2, CH), F32),
        ],
        n_in=2,
    )(spectrum, upright)

    middle = DEGREES * OWN
    after = along("x", own, -1)
    before = along("x", own, 1)
    low = along("y", own[:middle], 1)
    high = along("y", own[middle:], -1)
    parts = [(own, 0), (after, 1), (before, 3)]
    out = jnp.zeros((DEGREES, HELD, 2, CH), BF16)
    for value, step in parts:
        value = value.reshape(DEGREES, OWN, 2, CH)
        at = (colour + step) % SIDE * OWN
        out = lax.dynamic_update_slice(out, value, (0, at, 0, 0))
    at = (colour + 2) % SIDE * OWN
    for value, start in ((low, 0), (high, DEGREES // 2)):
        value = value.reshape(DEGREES // 2, OWN, 2, CH)
        out = lax.dynamic_update_slice(out, value, (start, at, 0, 0))
    return out


def solution(mesh):
    fine = Mesh(mesh.devices.reshape(SIDE, SIDE, LON), ("y", "x", "lon"))
    return jax.shard_map(
        on_device,
        mesh=fine,
        in_specs=(P(("y", "x"), "lon", None), P("lon", ("y", "x"), None)),
        out_specs=P(None, "lon", None, None),
        check_vma=False,
    )
```

```python
import jax
import jax.numpy as jnp
from jax import lax
from jax.experimental import pallas as pl
from jax.experimental.pallas import tpu as pltpu
from jax.sharding import Mesh, PartitionSpec as P

DEGREES = 672
ORDERS = 384
NLON = 1440
CH = 128
SIDE = 4
LAT = SIDE * SIDE
LON = 32
ROWS = 45
COLS = 45
PAD = 48
HELD = ORDERS // LON
OWN = HELD // SIDE
EXTRA = ROWS - LON
SENT = PAD + PAD // 2
BACK = 40
F32, BF16 = jnp.float32, jnp.bfloat16
HOPS = (0, 1, 3, 2)
SHIFTS = (0, 1, 3, 2)
VMEM_LIMIT = 20 * 1024 * 1024
CUTS = (0, 384, DEGREES)
TILES = (9, 7)


def call(body, out_shape, scratch=(), n_in=1):
    whole = pl.BlockSpec(memory_space=pltpu.VMEM)
    many = isinstance(out_shape, list)
    return pl.pallas_call(
        body,
        out_shape=out_shape,
        in_specs=[whole] * n_in,
        out_specs=[whole] * len(out_shape) if many else whole,
        scratch_shapes=list(scratch),
        compiler_params=pltpu.CompilerParams(vmem_limit_bytes=VMEM_LIMIT),
    )


def left_half(shape):
    return lax.broadcasted_iota(jnp.int32, shape, len(shape) - 1) < CH // 2


def pack_rows(grad_ref, out_ref, rows):
    rows[...] = jnp.zeros_like(rows)
    half = PAD // 2
    left = left_half((half, CH))
    for d in range(LON):
        rows[0:COLS, :] = grad_ref[d].astype(F32)
        out_ref[d, 0:PAD, :] = rows[...].astype(BF16)
    for extra in range(EXTRA):
        rows[0:COLS, :] = grad_ref[LON + extra].astype(F32)
        early, late = rows[0:half, :], rows[half:PAD, :]
        first = jnp.where(left, early, pltpu.roll(late, CH // 2, 1))
        second = jnp.where(left, pltpu.roll(early, CH // 2, 1), late)
        out_ref[2 * extra, PAD:SENT, :] = first.astype(BF16)
        out_ref[2 * extra + 1, PAD:SENT, :] = second.astype(BF16)
    for d in range(2 * EXTRA, LON):
        out_ref[d, PAD:SENT, :] = jnp.zeros((half, CH), BF16)


def spectrum_rows(x_ref, table_ref, out_ref, both):
    half = PAD // 2
    left = left_half((half, CH))
    for d in range(LON):
        at = d * PAD
        both[at : at + PAD, 0:CH] = x_ref[d, 0:PAD, :]
        packed = x_ref[d, PAD:SENT, :].astype(F32)
        early = jnp.where(left, packed, 0.0)
        late = jnp.where(left, pltpu.roll(packed, CH // 2, 1), 0.0)
        both[at : at + PAD, CH : 2 * CH] = jnp.concatenate([early, late], 0).astype(BF16)
    n = 2 * HELD
    found = jnp.dot(table_ref[...], both[...], preferred_element_type=F32)
    left8 = left_half((8, CH))
    for d in range(LON):
        whole = found[d * n : (d + 1) * n, 0:CH]
        part = found[d * n : (d + 1) * n, CH : 2 * CH]
        mixed = jnp.where(left8, part[0:8], pltpu.roll(part[16:24], CH // 2, 1))
        out_ref[d] = jnp.concatenate([whole, mixed, part[8:16]], 0).astype(BF16)


def turn_rows(r_ref, out_ref, flat):
    for d in range(LON):
        flat[d * BACK : (d + 1) * BACK, :] = r_ref[d].astype(F32)
    n = 2 * HELD
    left = left_half((16, CH))
    for order in range(HELD):
        colour, place = divmod(order, OWN)
        for part in range(2):
            i = part * HELD + order
            lanes = slice(part * CH, (part + 1) * CH)
            main = flat[pl.ds(i, LON, stride=BACK), :]
            at = n + (i if i < 16 else i - 16)
            even = flat[pl.ds(at, 16, stride=2 * BACK), :]
            odd = flat[pl.ds(BACK + at, 16, stride=2 * BACK), :]
            if i < 16:
                rest = jnp.where(left, even, pltpu.roll(odd, CH // 2, 1))
            else:
                rest = jnp.where(left, pltpu.roll(even, CH // 2, 1), odd)
            column = jnp.concatenate([main, rest], 0).astype(BF16)
            for t in range(LAT):
                if (t % SIDE + 2 * (t // SIDE)) % SIDE == colour:
                    out_ref[t, place, :, lanes] = column


def pack_legendre(legendre_ref, out_ref, wide):
    lon = lax.axis_index("lon")
    wide[...] = jnp.zeros_like(wide)
    degree = lax.broadcasted_iota(jnp.int32, (ROWS, DEGREES), 1)
    end = DEGREES // CH
    cut = CUTS[1] // CH
    for colour in range(SIDE):
        tails = jnp.zeros((PAD, CH), F32)
        for place in range(OWN):
            order = colour * OWN + place
            value = legendre_ref[order].astype(F32)
            wide[0:ROWS, 0:DEGREES] = jnp.where(degree >= lon * HELD + order, value, 0.0)
            for tile in range(end):
                if tile < cut:
                    at = place * cut + tile
                else:
                    at = TILES[0] + place * (end - cut) + tile - cut
                lanes = slice(tile * CH, (tile + 1) * CH)
                out_ref[colour, at] = wide[:, lanes].astype(BF16)
            tail = wide[:, end * CH : (end + 1) * CH]
            tails += pltpu.roll(tail, place * (DEGREES - end * CH), 1)
        out_ref[colour, sum(TILES) - 1] = tails.astype(BF16)


def turn_legendre(*refs):
    *parts, out_ref, tall = refs
    degrees = out_ref.shape[1]
    full, size = degrees // CH, degrees % CH
    for tile in range(parts[0].shape[1]):
        for hop, part in enumerate(parts):
            for shift in range(SIDE):
                at = (hop * SIDE + shift) * PAD
                tall[at : at + PAD, :] = part[shift, tile].astype(F32)
        turned = tall[...].T.astype(BF16)
        place, at = tile // full, tile % full * CH
        if place < OWN:
            out_ref[place, at : at + CH, :] = turned
        else:
            for place in range(OWN):
                out_ref[place, full * CH :, :] = turned[place * size : (place + 1) * size]


def legendre_sum(s_ref, p_ref, out_ref, gathered, spread):
    y, x = lax.axis_index("y"), lax.axis_index("x")
    for hop, step in enumerate(HOPS):
        row = lax.rem(y + (SIDE - step), SIDE)
        for shift in range(SIDE):
            column = lax.rem(x + (3 * SIDE - 2 * step - SHIFTS[shift]), SIDE)
            at = (hop * SIDE + shift) * PAD
            for place in range(OWN):
                gathered[place, at : at + PAD, :] = s_ref[row * SIDE + column, place]
    for place in range(OWN):
        found = jnp.dot(p_ref[place], gathered[place], preferred_element_type=F32)
        for part in range(2):
            rows = pl.ds(2 * place + part, p_ref.shape[1], stride=2 * OWN)
            spread[rows, :] = found[:, part * CH : (part + 1) * CH]
    out_ref[...] = spread[...].astype(BF16)


def fourier_factors():
    rows = jnp.arange(2 * ORDERS, dtype=jnp.int32)[None, :]
    part = rows % (2 * HELD) // HELD
    order = rows // (2 * HELD) * HELD + rows % HELD
    device = jnp.arange(LON, dtype=jnp.int32)[:, None]
    within = jnp.arange(PAD, dtype=jnp.int32)[:, None]
    weight = jnp.where(order == 0, 1.0, 2.0).astype(F32) / jnp.sqrt(F32(NLON))
    weight = jnp.where(within < COLS, weight, 0.0)
    turn = 2.0 * jnp.pi / NLON
    first = (device * COLS * order % NLON).astype(F32) * turn
    rest = ((within * order + part * (NLON // 4)) % NLON).astype(F32) * turn
    return jnp.cos(first), jnp.sin(first), weight * jnp.cos(rest), weight * jnp.sin(rest)


def fourier_table(cos_a, sin_a, cos_b, sin_b, out_ref, tall):
    for d in range(LON):
        row = slice(d, d + 1)
        tall[d * PAD : (d + 1) * PAD, :] = (
            cos_a[row, :] * cos_b[...] - sin_a[row, :] * sin_b[...]
        )
    out_ref[...] = tall[...].T.astype(BF16)


def along(axis, value, step):
    return lax.ppermute(value, axis, [(i, (i + step) % SIDE) for i in range(SIDE)])


def same_colour(value, step):
    pairs = []
    for y in range(SIDE):
        for x in range(SIDE):
            to = (y + step) % SIDE * SIDE + (x + 2 * step) % SIDE
            pairs.append((y * SIDE + x, to))
    return lax.ppermute(value, ("y", "x"), pairs)


def on_device(grad_field, legendre):
    colour = (lax.axis_index("x") + 2 * lax.axis_index("y")) % SIDE
    struct = jax.ShapeDtypeStruct

    packed = call(
        pack_rows, struct((LON, SENT, CH), BF16), [pltpu.VMEM((PAD, CH), F32)]
    )(grad_field)
    row_columns = lax.all_to_all(packed, "lon", 0, 0, tiled=True)

    masked = call(
        pack_legendre,
        struct((SIDE, sum(TILES), PAD, CH), BF16),
        [pltpu.VMEM((PAD, 768), F32)],
    )(legendre)
    line = [lax.dynamic_index_in_dim(masked, colour, 0, keepdims=False)]
    for step in SHIFTS[1:]:
        theirs = lax.dynamic_index_in_dim(masked, (colour + step) % SIDE, 0, keepdims=False)
        line.append(along("x", theirs, step))
    table = call(
        fourier_table,
        struct((2 * ORDERS, LON * PAD), BF16),
        [pltpu.VMEM((LON * PAD, 2 * ORDERS), F32)],
        n_in=4,
    )(*fourier_factors())
    first = jnp.stack([part[: TILES[0]] for part in line])
    second = jnp.stack([part[TILES[0] :] for part in line])
    one, three, two = (same_colour(first, step) for step in HOPS[1:])
    one_b, three_b, two_b = (same_colour(second, step) for step in HOPS[1:])
    row_columns, one = lax.optimization_barrier((row_columns, one))

    returned = call(
        spectrum_rows,
        struct((LON, BACK, CH), BF16),
        [pltpu.VMEM((LON * PAD, 2 * CH), BF16)],
        n_in=2,
    )(row_columns, table)
    by_sender = lax.all_to_all(returned, "lon", 0, 0, tiled=True)
    by_sender, three, two, one_b = lax.optimization_barrier((by_sender, three, two, one_b))
    turned = call(
        turn_rows,
        struct((LAT, OWN, PAD, 2 * CH), BF16),
        [pltpu.VMEM((LON * BACK, CH), F32)],
    )(by_sender)
    spectrum = lax.all_to_all(turned, ("y", "x"), 0, 0, tiled=True)

    sums = []
    for span, blocks in enumerate(
        [(first, one, three, two), (second, one_b, three_b, two_b)]
    ):
        degrees = CUTS[span + 1] - CUTS[span]
        upright = call(
            turn_legendre,
            struct((OWN, degrees, LAT * PAD), BF16),
            [pltpu.VMEM((LAT * PAD, CH), F32)],
            n_in=SIDE,
        )(*blocks)
        found = call(
            legendre_sum,
            struct((degrees * OWN * 2, CH), BF16),
            [
                pltpu.VMEM((OWN, LAT * PAD, 2 * CH), BF16),
                pltpu.VMEM((degrees * OWN * 2, CH), F32),
            ],
            n_in=2,
        )(spectrum, upright)
        sums.append(found)

    parts = []
    for span, found in enumerate(sums):
        parts.append((span, 1, along("x", found, -1)))
        parts.append((span, 3, along("x", found, 1)))
        parts.append((span, 2, along("y", found, 1 - 2 * span)))
    parts = [(0, 0, sums[0]), (1, 0, sums[1])] + sorted(parts, key=lambda p: (p[0], p[1] != 2))
    out = jnp.zeros((DEGREES, HELD, 2, CH), BF16)
    for span, step, value in parts:
        value = value.reshape(-1, OWN, 2, CH)
        at = (colour + step) % SIDE * OWN
        out = lax.dynamic_update_slice(out, value, (CUTS[span], at, 0, 0))
    return out


def solution(mesh):
    fine = Mesh(mesh.devices.reshape(SIDE, SIDE, LON), ("y", "x", "lon"))
    return jax.shard_map(
        on_device,
        mesh=fine,
        in_specs=(P(("y", "x"), "lon", None), P("lon", ("y", "x"), None)),
        out_specs=P(None, "lon", None, None),
        check_vma=False,
    )
```

```python
import jax
import jax.numpy as jnp
from jax import lax
from jax.experimental import pallas as pl
from jax.experimental.pallas import tpu as pltpu
from jax.sharding import Mesh, PartitionSpec as P

DEGREES = 672
ORDERS = 384
NLON = 1440
CH = 128
SIDE = 4
LAT = SIDE * SIDE
LON = 32
ROWS = 45
COLS = 45
PAD = 48
HELD = ORDERS // LON
OWN = HELD // SIDE
EXTRA = ROWS - LON
SENT = PAD + PAD // 2
BACK = 40
F32, BF16 = jnp.float32, jnp.bfloat16
HOPS = (0, 1, 3, 2)
SHIFTS = (0, 1, 3, 2)
MIB = 1024 * 1024
FULL = DEGREES // CH
TAIL = DEGREES % CH
TILES = OWN * FULL + 1

LONG = pl.CostEstimate(flops=10**11, transcendentals=0, bytes_accessed=10**9)


def call(body, out_shape, scratch=(), n_in=1, vmem=8, cost=None):
    whole = pl.BlockSpec(memory_space=pltpu.VMEM)
    many = isinstance(out_shape, list)
    return pl.pallas_call(
        body,
        out_shape=out_shape,
        in_specs=[whole] * n_in,
        out_specs=[whole] * len(out_shape) if many else whole,
        scratch_shapes=list(scratch),
        cost_estimate=cost,
        compiler_params=pltpu.CompilerParams(vmem_limit_bytes=vmem * MIB),
    )


def left_half(shape):
    return lax.broadcasted_iota(jnp.int32, shape, len(shape) - 1) < CH // 2


def pack_rows(grad_ref, out_ref, rows):
    rows[...] = jnp.zeros_like(rows)
    half = PAD // 2
    left = left_half((half, CH))
    for d in range(LON):
        rows[0:COLS, :] = grad_ref[d].astype(F32)
        out_ref[d, 0:PAD, :] = rows[...].astype(BF16)
    for extra in range(EXTRA):
        rows[0:COLS, :] = grad_ref[LON + extra].astype(F32)
        early, late = rows[0:half, :], rows[half:PAD, :]
        first = jnp.where(left, early, pltpu.roll(late, CH // 2, 1))
        second = jnp.where(left, pltpu.roll(early, CH // 2, 1), late)
        out_ref[2 * extra, PAD:SENT, :] = first.astype(BF16)
        out_ref[2 * extra + 1, PAD:SENT, :] = second.astype(BF16)
    for d in range(2 * EXTRA, LON):
        out_ref[d, PAD:SENT, :] = jnp.zeros((half, CH), BF16)


def spectrum_rows(x_ref, table_ref, out_ref, both):
    half = PAD // 2
    left = left_half((half, CH))
    for d in range(LON):
        at = d * PAD
        both[at : at + PAD, 0:CH] = x_ref[d, 0:PAD, :]
        packed = x_ref[d, PAD:SENT, :].astype(F32)
        early = jnp.where(left, packed, 0.0)
        late = jnp.where(left, pltpu.roll(packed, CH // 2, 1), 0.0)
        both[at : at + PAD, CH : 2 * CH] = jnp.concatenate([early, late], 0).astype(BF16)
    n = 2 * HELD
    found = jnp.dot(table_ref[...], both[...], preferred_element_type=F32)
    left8 = left_half((8, CH))
    for d in range(LON):
        whole = found[d * n : (d + 1) * n, 0:CH]
        part = found[d * n : (d + 1) * n, CH : 2 * CH]
        mixed = jnp.where(left8, part[0:8], pltpu.roll(part[16:24], CH // 2, 1))
        out_ref[d] = jnp.concatenate([whole, mixed, part[8:16]], 0).astype(BF16)


def turn_rows(r_ref, out_ref, flat):
    for d in range(LON):
        flat[d * BACK : (d + 1) * BACK, :] = r_ref[d].astype(F32)
    n = 2 * HELD
    left = left_half((16, CH))
    for order in range(HELD):
        colour, place = divmod(order, OWN)
        for part in range(2):
            i = part * HELD + order
            lanes = slice(part * CH, (part + 1) * CH)
            main = flat[pl.ds(i, LON, stride=BACK), :]
            at = n + (i if i < 16 else i - 16)
            even = flat[pl.ds(at, 16, stride=2 * BACK), :]
            odd = flat[pl.ds(BACK + at, 16, stride=2 * BACK), :]
            if i < 16:
                rest = jnp.where(left, even, pltpu.roll(odd, CH // 2, 1))
            else:
                rest = jnp.where(left, pltpu.roll(even, CH // 2, 1), odd)
            column = jnp.concatenate([main, rest], 0).astype(BF16)
            for t in range(LAT):
                if (t % SIDE + 2 * (t // SIDE)) % SIDE == colour:
                    out_ref[t, place, :, lanes] = column


def pack_legendre(legendre_ref, out_ref, wide):
    lon = lax.axis_index("lon")
    wide[...] = jnp.zeros_like(wide)
    degree = lax.broadcasted_iota(jnp.int32, (ROWS, DEGREES), 1)
    for colour in range(SIDE):
        tails = jnp.zeros((PAD, CH), F32)
        for place in range(OWN):
            order = colour * OWN + place
            value = legendre_ref[order].astype(F32)
            wide[0:ROWS, 0:DEGREES] = jnp.where(degree >= lon * HELD + order, value, 0.0)
            for tile in range(FULL):
                lanes = slice(tile * CH, (tile + 1) * CH)
                out_ref[colour, place * FULL + tile] = wide[:, lanes].astype(BF16)
            tail = wide[:, FULL * CH : (FULL + 1) * CH]
            tails += pltpu.roll(tail, place * TAIL, 1)
        out_ref[colour, TILES - 1] = tails.astype(BF16)


def turn_legendre(*refs):
    *parts, out_ref, tall = refs
    for tile in range(TILES):
        for hop, part in enumerate(parts):
            for shift in range(SIDE):
                at = (hop * SIDE + shift) * PAD
                tall[at : at + PAD, :] = part[shift, tile].astype(F32)
        turned = tall[...].T.astype(BF16)
        if tile == TILES - 1:
            for place in range(OWN):
                rows = slice(place * TAIL, (place + 1) * TAIL)
                out_ref[place, FULL * CH : DEGREES, :] = turned[rows]
        else:
            place, at = tile // FULL, tile % FULL * CH
            out_ref[place, at : at + CH, :] = turned


def legendre_sum(s_ref, p_ref, out_ref, gathered, spread):
    y, x = lax.axis_index("y"), lax.axis_index("x")
    for hop, step in enumerate(HOPS):
        row = lax.rem(y + (SIDE - step), SIDE)
        for shift in range(SIDE):
            column = lax.rem(x + (3 * SIDE - 2 * step - SHIFTS[shift]), SIDE)
            at = (hop * SIDE + shift) * PAD
            for place in range(OWN):
                gathered[place, at : at + PAD, :] = s_ref[row * SIDE + column, place]
    for place in range(OWN):
        found = jnp.dot(p_ref[place], gathered[place], preferred_element_type=F32)
        for part in range(2):
            rows = pl.ds(2 * place + part, DEGREES, stride=2 * OWN)
            spread[rows, :] = found[:, part * CH : (part + 1) * CH]
    out_ref[...] = spread[...].astype(BF16)


def fourier_factors():
    rows = jnp.arange(2 * ORDERS, dtype=jnp.int32)[None, :]
    part = rows % (2 * HELD) // HELD
    order = rows // (2 * HELD) * HELD + rows % HELD
    device = jnp.arange(LON, dtype=jnp.int32)[:, None]
    within = jnp.arange(PAD, dtype=jnp.int32)[:, None]
    weight = jnp.where(order == 0, 1.0, 2.0).astype(F32) / jnp.sqrt(F32(NLON))
    weight = jnp.where(within < COLS, weight, 0.0)
    turn = 2.0 * jnp.pi / NLON
    first = (device * COLS * order % NLON).astype(F32) * turn
    rest = ((within * order + part * (NLON // 4)) % NLON).astype(F32) * turn
    return jnp.cos(first), jnp.sin(first), weight * jnp.cos(rest), weight * jnp.sin(rest)


def fourier_table(cos_a, sin_a, cos_b, sin_b, out_ref, tall):
    for d in range(LON):
        row = slice(d, d + 1)
        tall[d * PAD : (d + 1) * PAD, :] = (
            cos_a[row, :] * cos_b[...] - sin_a[row, :] * sin_b[...]
        )
    out_ref[...] = tall[...].T.astype(BF16)


def along(axis, value, step):
    return lax.ppermute(value, axis, [(i, (i + step) % SIDE) for i in range(SIDE)])


def same_colour(value, step):
    pairs = []
    for y in range(SIDE):
        for x in range(SIDE):
            to = (y + step) % SIDE * SIDE + (x + 2 * step) % SIDE
            pairs.append((y * SIDE + x, to))
    return lax.ppermute(value, ("y", "x"), pairs)


def on_device(grad_field, legendre):
    colour = (lax.axis_index("x") + 2 * lax.axis_index("y")) % SIDE
    struct = jax.ShapeDtypeStruct

    packed = call(
        pack_rows, struct((LON, SENT, CH), BF16), [pltpu.VMEM((PAD, CH), F32)]
    )(grad_field)
    row_columns = lax.all_to_all(packed, "lon", 0, 0, tiled=True)

    masked = call(
        pack_legendre,
        struct((SIDE, TILES, PAD, CH), BF16),
        [pltpu.VMEM((PAD, (FULL + 1) * CH), F32)],
    )(legendre)
    line = [lax.dynamic_index_in_dim(masked, colour, 0, keepdims=False)]
    for step in SHIFTS[1:]:
        theirs = lax.dynamic_index_in_dim(masked, (colour + step) % SIDE, 0, keepdims=False)
        line.append(along("x", theirs, step))
    table = call(
        fourier_table,
        struct((2 * ORDERS, LON * PAD), BF16),
        [pltpu.VMEM((LON * PAD, 2 * ORDERS), F32)],
        n_in=4,
        vmem=16,
    )(*fourier_factors())
    line = jnp.stack(line)
    lines = [line] + [same_colour(line, step) for step in HOPS[1:]]
    upright = call(
        turn_legendre,
        struct((OWN, DEGREES, LAT * PAD), BF16),
        [pltpu.VMEM((LAT * PAD, CH), F32)],
        n_in=SIDE,
        cost=LONG,
    )(*lines)

    returned = call(
        spectrum_rows,
        struct((LON, BACK, CH), BF16),
        [pltpu.VMEM((LON * PAD, 2 * CH), BF16)],
        n_in=2,
    )(row_columns, table)
    by_sender = lax.all_to_all(returned, "lon", 0, 0, tiled=True)
    by_sender, upright = lax.optimization_barrier((by_sender, upright))
    turned = call(
        turn_rows,
        struct((LAT, OWN, PAD, 2 * CH), BF16),
        [pltpu.VMEM((LON * BACK, CH), F32)],
    )(by_sender)
    spectrum = lax.all_to_all(turned, ("y", "x"), 0, 0, tiled=True)

    middle = DEGREES * OWN
    own = call(
        legendre_sum,
        struct((2 * middle, CH), BF16),
        [
            pltpu.VMEM((OWN, LAT * PAD, 2 * CH), BF16),
            pltpu.VMEM((2 * middle, CH), F32),
        ],
        n_in=2,
    )(spectrum, upright)

    after = along("x", own, -1)
    before = along("x", own, 1)
    low = along("y", own[:middle], 1)
    high = along("y", own[middle:], -1)
    parts = [(own, 0, 0), (low, 2, 0), (high, 2, DEGREES // 2), (after, 1, 0), (before, 3, 0)]
    out = jnp.zeros((DEGREES, HELD, 2, CH), BF16)
    for value, step, start in parts:
        value = value.reshape(-1, OWN, 2, CH)
        at = (colour + step) % SIDE * OWN
        out = lax.dynamic_update_slice(out, value, (start, at, 0, 0))
    return out


def solution(mesh):
    fine = Mesh(mesh.devices.reshape(SIDE, SIDE, LON), ("y", "x", "lon"))
    return jax.shard_map(
        on_device,
        mesh=fine,
        in_specs=(P(("y", "x"), "lon", None), P("lon", ("y", "x"), None)),
        out_specs=P(None, "lon", None, None),
        check_vma=False,
    )
```

```python
import jax
import jax.numpy as jnp
from jax import lax
from jax.experimental import pallas as pl
from jax.experimental.pallas import tpu as pltpu
from jax.sharding import Mesh, PartitionSpec as P

DEGREES = 672
ORDERS = 384
NLON = 1440
CH = 128
SIDE = 4
LAT = SIDE * SIDE
LON = 32
ROWS = 45
COLS = 45
PAD = 48
HELD = ORDERS // LON
OWN = HELD // SIDE
EXTRA = ROWS - LON
SENT = PAD + PAD // 2
BACK = 40
F32, BF16 = jnp.float32, jnp.bfloat16
HOPS = (0, 1, 3, 2)
NEAR = ((0, 0), (-1, 0), (0, -1), (0, 1))
MIB = 1024 * 1024
FULL = DEGREES // CH
TAIL = DEGREES % CH
TILES = OWN * FULL + 1

LONG = pl.CostEstimate(flops=10**11, transcendentals=0, bytes_accessed=10**9)


def call(body, out_shape, scratch=(), n_in=1, vmem=8, cost=None):
    whole = pl.BlockSpec(memory_space=pltpu.VMEM)
    many = isinstance(out_shape, list)
    return pl.pallas_call(
        body,
        out_shape=out_shape,
        in_specs=[whole] * n_in,
        out_specs=[whole] * len(out_shape) if many else whole,
        scratch_shapes=list(scratch),
        cost_estimate=cost,
        compiler_params=pltpu.CompilerParams(vmem_limit_bytes=vmem * MIB),
    )


def left_half(shape):
    return lax.broadcasted_iota(jnp.int32, shape, len(shape) - 1) < CH // 2


def pack_rows(grad_ref, out_ref, rows):
    rows[...] = jnp.zeros_like(rows)
    half = PAD // 2
    left = left_half((half, CH))
    for d in range(LON):
        rows[0:COLS, :] = grad_ref[d].astype(F32)
        out_ref[d, 0:PAD, :] = rows[...].astype(BF16)
    for extra in range(EXTRA):
        rows[0:COLS, :] = grad_ref[LON + extra].astype(F32)
        early, late = rows[0:half, :], rows[half:PAD, :]
        first = jnp.where(left, early, pltpu.roll(late, CH // 2, 1))
        second = jnp.where(left, pltpu.roll(early, CH // 2, 1), late)
        out_ref[2 * extra, PAD:SENT, :] = first.astype(BF16)
        out_ref[2 * extra + 1, PAD:SENT, :] = second.astype(BF16)
    for d in range(2 * EXTRA, LON):
        out_ref[d, PAD:SENT, :] = jnp.zeros((half, CH), BF16)


def spectrum_rows(x_ref, table_ref, out_ref, both):
    half = PAD // 2
    left = left_half((half, CH))
    for d in range(LON):
        at = d * PAD
        both[at : at + PAD, 0:CH] = x_ref[d, 0:PAD, :]
        packed = x_ref[d, PAD:SENT, :].astype(F32)
        early = jnp.where(left, packed, 0.0)
        late = jnp.where(left, pltpu.roll(packed, CH // 2, 1), 0.0)
        both[at : at + PAD, CH : 2 * CH] = jnp.concatenate([early, late], 0).astype(BF16)
    n = 2 * HELD
    found = jnp.dot(table_ref[...], both[...], preferred_element_type=F32)
    left8 = left_half((8, CH))
    for d in range(LON):
        whole = found[d * n : (d + 1) * n, 0:CH]
        part = found[d * n : (d + 1) * n, CH : 2 * CH]
        mixed = jnp.where(left8, part[0:8], pltpu.roll(part[16:24], CH // 2, 1))
        out_ref[d] = jnp.concatenate([whole, mixed, part[8:16]], 0).astype(BF16)


def turn_rows(r_ref, out_ref, flat):
    for d in range(LON):
        flat[d * BACK : (d + 1) * BACK, :] = r_ref[d].astype(F32)
    n = 2 * HELD
    left = left_half((16, CH))
    for order in range(HELD):
        colour, place = divmod(order, OWN)
        for part in range(2):
            i = part * HELD + order
            lanes = slice(part * CH, (part + 1) * CH)
            main = flat[pl.ds(i, LON, stride=BACK), :]
            at = n + (i if i < 16 else i - 16)
            even = flat[pl.ds(at, 16, stride=2 * BACK), :]
            odd = flat[pl.ds(BACK + at, 16, stride=2 * BACK), :]
            if i < 16:
                rest = jnp.where(left, even, pltpu.roll(odd, CH // 2, 1))
            else:
                rest = jnp.where(left, pltpu.roll(even, CH // 2, 1), odd)
            column = jnp.concatenate([main, rest], 0).astype(BF16)
            for t in range(LAT):
                if (t % SIDE + 2 * (t // SIDE)) % SIDE == colour:
                    out_ref[t, place, :, lanes] = column


def pack_legendre(legendre_ref, out_ref, wide):
    lon = lax.axis_index("lon")
    wide[...] = jnp.zeros_like(wide)
    degree = lax.broadcasted_iota(jnp.int32, (ROWS, DEGREES), 1)
    for colour in range(SIDE):
        tails = jnp.zeros((PAD, CH), F32)
        for place in range(OWN):
            order = colour * OWN + place
            value = legendre_ref[order].astype(F32)
            wide[0:ROWS, 0:DEGREES] = jnp.where(degree >= lon * HELD + order, value, 0.0)
            for tile in range(FULL):
                lanes = slice(tile * CH, (tile + 1) * CH)
                out_ref[colour, place * FULL + tile] = wide[:, lanes].astype(BF16)
            tail = wide[:, FULL * CH : (FULL + 1) * CH]
            tails += pltpu.roll(tail, place * TAIL, 1)
        out_ref[colour, TILES - 1] = tails.astype(BF16)


def turn_legendre(*refs):
    *parts, out_ref, tall = refs
    for tile in range(TILES):
        for hop, part in enumerate(parts):
            for shift in range(SIDE):
                at = (hop * SIDE + shift) * PAD
                tall[at : at + PAD, :] = part[shift, tile].astype(F32)
        turned = tall[...].T.astype(BF16)
        if tile == TILES - 1:
            for place in range(OWN):
                rows = slice(place * TAIL, (place + 1) * TAIL)
                out_ref[place, FULL * CH : DEGREES, :] = turned[rows]
        else:
            place, at = tile // FULL, tile % FULL * CH
            out_ref[place, at : at + CH, :] = turned


def legendre_sum(s_ref, p_ref, out_ref, gathered, spread):
    y, x = lax.axis_index("y"), lax.axis_index("x")
    for hop, step in enumerate(HOPS):
        for shift, (rows, columns) in enumerate(NEAR):
            row = lax.rem(y + (2 * SIDE - step + rows), SIDE)
            column = lax.rem(x + (3 * SIDE - 2 * step + columns), SIDE)
            at = (hop * SIDE + shift) * PAD
            for place in range(OWN):
                gathered[place, at : at + PAD, :] = s_ref[row * SIDE + column, place]
    for place in range(OWN):
        found = jnp.dot(p_ref[place], gathered[place], preferred_element_type=F32)
        for part in range(2):
            rows = pl.ds(2 * place + part, DEGREES, stride=2 * OWN)
            spread[rows, :] = found[:, part * CH : (part + 1) * CH]
    out_ref[...] = spread[...].astype(BF16)


def fourier_factors():
    rows = jnp.arange(2 * ORDERS, dtype=jnp.int32)[None, :]
    part = rows % (2 * HELD) // HELD
    order = rows // (2 * HELD) * HELD + rows % HELD
    device = jnp.arange(LON, dtype=jnp.int32)[:, None]
    within = jnp.arange(PAD, dtype=jnp.int32)[:, None]
    weight = jnp.where(order == 0, 1.0, 2.0).astype(F32) / jnp.sqrt(F32(NLON))
    weight = jnp.where(within < COLS, weight, 0.0)
    turn = 2.0 * jnp.pi / NLON
    first = (device * COLS * order % NLON).astype(F32) * turn
    rest = ((within * order + part * (NLON // 4)) % NLON).astype(F32) * turn
    return jnp.cos(first), jnp.sin(first), weight * jnp.cos(rest), weight * jnp.sin(rest)


def fourier_table(cos_a, sin_a, cos_b, sin_b, out_ref, tall):
    for d in range(LON):
        row = slice(d, d + 1)
        tall[d * PAD : (d + 1) * PAD, :] = (
            cos_a[row, :] * cos_b[...] - sin_a[row, :] * sin_b[...]
        )
    out_ref[...] = tall[...].T.astype(BF16)


def along(axis, value, step):
    return lax.ppermute(value, axis, [(i, (i + step) % SIDE) for i in range(SIDE)])


def same_colour(value, step):
    pairs = []
    for y in range(SIDE):
        for x in range(SIDE):
            to = (y + step) % SIDE * SIDE + (x + 2 * step) % SIDE
            pairs.append((y * SIDE + x, to))
    return lax.ppermute(value, ("y", "x"), pairs)


def on_device(grad_field, legendre):
    colour = (lax.axis_index("x") + 2 * lax.axis_index("y")) % SIDE
    struct = jax.ShapeDtypeStruct

    packed = call(
        pack_rows, struct((LON, SENT, CH), BF16), [pltpu.VMEM((PAD, CH), F32)]
    )(grad_field)
    row_columns = lax.all_to_all(packed, "lon", 0, 0, tiled=True)

    masked = call(
        pack_legendre,
        struct((SIDE, TILES, PAD, CH), BF16),
        [pltpu.VMEM((PAD, (FULL + 1) * CH), F32)],
    )(legendre)
    line = [lax.dynamic_index_in_dim(masked, colour, 0, keepdims=False)]
    for rows, columns in NEAR[1:]:
        theirs = (colour - 2 * rows - columns) % SIDE
        theirs = lax.dynamic_index_in_dim(masked, theirs, 0, keepdims=False)
        line.append(along("y" if rows else "x", theirs, -rows - columns))
    line = jnp.stack(line)
    table = call(
        fourier_table,
        struct((2 * ORDERS, LON * PAD), BF16),
        [pltpu.VMEM((LON * PAD, 2 * ORDERS), F32)],
        n_in=4,
        vmem=16,
    )(*fourier_factors())
    line, table = lax.optimization_barrier((line, table))
    lines = [line] + [same_colour(line, step) for step in HOPS[1:]]
    upright = call(
        turn_legendre,
        struct((OWN, DEGREES, LAT * PAD), BF16),
        [pltpu.VMEM((LAT * PAD, CH), F32)],
        n_in=SIDE,
        cost=LONG,
    )(*lines)

    returned = call(
        spectrum_rows,
        struct((LON, BACK, CH), BF16),
        [pltpu.VMEM((LON * PAD, 2 * CH), BF16)],
        n_in=2,
    )(row_columns, table)
    by_sender = lax.all_to_all(returned, "lon", 0, 0, tiled=True)
    by_sender, upright = lax.optimization_barrier((by_sender, upright))
    turned = call(
        turn_rows,
        struct((LAT, OWN, PAD, 2 * CH), BF16),
        [pltpu.VMEM((LON * BACK, CH), F32)],
    )(by_sender)
    spectrum = lax.all_to_all(turned, ("y", "x"), 0, 0, tiled=True)

    middle = DEGREES * OWN
    own = call(
        legendre_sum,
        struct((2 * middle, CH), BF16),
        [
            pltpu.VMEM((OWN, LAT * PAD, 2 * CH), BF16),
            pltpu.VMEM((2 * middle, CH), F32),
        ],
        n_in=2,
    )(spectrum, upright)

    after = along("x", own, -1)
    before = along("x", own, 1)
    low = along("y", own[:middle], 1)
    high = along("y", own[middle:], -1)
    parts = [(own, 0, 0), (low, 2, 0), (high, 2, DEGREES // 2), (after, 1, 0), (before, 3, 0)]
    out = jnp.zeros((DEGREES, HELD, 2, CH), BF16)
    for value, step, start in parts:
        value = value.reshape(-1, OWN, 2, CH)
        at = (colour + step) % SIDE * OWN
        out = lax.dynamic_update_slice(out, value, (start, at, 0, 0))
    return out


def solution(mesh):
    fine = Mesh(mesh.devices.reshape(SIDE, SIDE, LON), ("y", "x", "lon"))
    return jax.shard_map(
        on_device,
        mesh=fine,
        in_specs=(P(("y", "x"), "lon", None), P("lon", ("y", "x"), None)),
        out_specs=P(None, "lon", None, None),
        check_vma=False,
    )
```

```python
import jax
import jax.numpy as jnp
from jax import lax
from jax.experimental import pallas as pl
from jax.experimental.pallas import tpu as pltpu
from jax.sharding import Mesh, PartitionSpec as P

DEGREES = 672
ORDERS = 384
NLON = 1440
CH = 128
SIDE = 4
LAT = SIDE * SIDE
LON = 32
ROWS = 45
COLS = 45
PAD = 48
HELD = ORDERS // LON
OWN = HELD // SIDE
EXTRA = ROWS - LON
HALF = (COLS + 1) // 2
SENT = COLS + HALF
BACK = 36
F32, BF16 = jnp.float32, jnp.bfloat16
HOPS = (0, 3, 1, 2)
NEAR = ((0, 0), (-1, 0), (0, -1), (0, 1))
MIB = 1024 * 1024
FULL = DEGREES // CH
TAIL = DEGREES % CH
TILES = OWN * FULL + 1

LONG = pl.CostEstimate(flops=10**11, transcendentals=0, bytes_accessed=10**9)


def call(body, out_shape, scratch=(), n_in=1, vmem=8, cost=None):
    whole = pl.BlockSpec(memory_space=pltpu.VMEM)
    many = isinstance(out_shape, list)
    return pl.pallas_call(
        body,
        out_shape=out_shape,
        in_specs=[whole] * n_in,
        out_specs=[whole] * len(out_shape) if many else whole,
        scratch_shapes=list(scratch),
        cost_estimate=cost,
        compiler_params=pltpu.CompilerParams(vmem_limit_bytes=vmem * MIB),
    )


def left_half(shape):
    return lax.broadcasted_iota(jnp.int32, shape, len(shape) - 1) < CH // 2


def pack_rows(grad_ref, out_ref, rows, flat):
    rows[...] = jnp.zeros_like(rows)
    left = left_half((HALF, CH))
    for d in range(2 * EXTRA, LON):
        flat[d * SENT + COLS : (d + 1) * SENT, :] = jnp.zeros((HALF, CH), F32)
    for row in range(ROWS):
        if row < LON:
            flat[row * SENT : row * SENT + COLS, :] = grad_ref[row].astype(F32)
        else:
            rows[0:COLS, :] = grad_ref[row].astype(F32)
            early, late = rows[0:HALF, :], rows[HALF : 2 * HALF, :]
            first = jnp.where(left, early, pltpu.roll(late, CH // 2, 1))
            second = jnp.where(left, pltpu.roll(early, CH // 2, 1), late)
            at = 2 * (row - LON) * SENT
            flat[at + COLS : at + SENT, :] = first
            flat[at + SENT + COLS : at + 2 * SENT, :] = second
    out_ref[...] = flat[...].astype(BF16)


def spectrum_rows(x_ref, table_ref, out_ref, both, flat, got, rows):
    got[0 : LON * SENT, :] = x_ref[...].astype(F32)
    got[LON * SENT :, :] = jnp.zeros_like(got[LON * SENT :, :])
    rows[...] = jnp.zeros_like(rows)
    half = PAD // 2
    left = left_half((half, CH))
    for d in range(LON):
        at = d * PAD
        both[at : at + PAD, 0:CH] = got[d * SENT : d * SENT + PAD, :].astype(BF16)
        packed = got[d * SENT + COLS : d * SENT + COLS + half, :]
        rows[0:half, :] = jnp.where(left, packed, 0.0)
        rows[HALF : HALF + half, :] = jnp.where(left, pltpu.roll(packed, CH // 2, 1), 0.0)
        both[at : at + PAD, CH : 2 * CH] = rows[...].astype(BF16)
    n = 2 * HELD
    found = jnp.dot(table_ref[...], both[...], preferred_element_type=F32)
    for d in range(LON):
        at = d * BACK
        flat[at : at + n, :] = found[d * n : (d + 1) * n, 0:CH]
        part = found[d * n : (d + 1) * n, CH : 2 * CH]
        high = pltpu.roll(part, CH // 2, 1)[HELD:n]
        flat[at + n : at + BACK, :] = jnp.where(left_half((HELD, CH)), part[0:HELD], high)
    out_ref[...] = flat[...].astype(BF16)


def turn_rows(r_ref, out_ref, flat):
    flat[...] = r_ref[...].astype(F32)
    n = 2 * HELD
    left = left_half((16, CH))
    for order in range(HELD):
        colour, place = divmod(order, OWN)
        for part in range(2):
            i = part * HELD + order
            lanes = slice(part * CH, (part + 1) * CH)
            main = flat[pl.ds(i, LON, stride=BACK), :]
            at = n + i % HELD
            even = flat[pl.ds(at, 16, stride=2 * BACK), :]
            odd = flat[pl.ds(BACK + at, 16, stride=2 * BACK), :]
            if part == 0:
                rest = jnp.where(left, even, pltpu.roll(odd, CH // 2, 1))
            else:
                rest = jnp.where(left, pltpu.roll(even, CH // 2, 1), odd)
            column = jnp.concatenate([main, rest], 0).astype(BF16)
            for t in range(LAT):
                if (t % SIDE + 2 * (t // SIDE)) % SIDE == colour:
                    out_ref[t, place, :, lanes] = column


def pack_legendre(legendre_ref, out_ref, wide):
    lon = lax.axis_index("lon")
    wide[...] = jnp.zeros_like(wide)
    degree = lax.broadcasted_iota(jnp.int32, (ROWS, DEGREES), 1)
    for colour in range(SIDE):
        tails = jnp.zeros((PAD, CH), F32)
        for place in range(OWN):
            order = colour * OWN + place
            value = legendre_ref[order].astype(F32)
            wide[0:ROWS, 0:DEGREES] = jnp.where(degree >= lon * HELD + order, value, 0.0)
            for tile in range(FULL):
                lanes = slice(tile * CH, (tile + 1) * CH)
                out_ref[colour, place * FULL + tile] = wide[:, lanes].astype(BF16)
            tail = wide[:, FULL * CH : (FULL + 1) * CH]
            tails += pltpu.roll(tail, place * TAIL, 1)
        out_ref[colour, TILES - 1] = tails.astype(BF16)


def turn_legendre(*refs):
    *parts, out_ref, tall = refs
    for tile in range(TILES):
        for hop, part in enumerate(parts):
            for shift in range(SIDE):
                at = (hop * SIDE + shift) * PAD
                tall[at : at + PAD, :] = part[shift, tile].astype(F32)
        turned = tall[...].T.astype(BF16)
        if tile == TILES - 1:
            for place in range(OWN):
                rows = slice(place * TAIL, (place + 1) * TAIL)
                out_ref[place, FULL * CH : DEGREES, :] = turned[rows]
        else:
            place, at = tile // FULL, tile % FULL * CH
            out_ref[place, at : at + CH, :] = turned


def legendre_sum(s_ref, p_ref, out_ref, gathered, spread):
    y, x = lax.axis_index("y"), lax.axis_index("x")
    for hop, step in enumerate(HOPS):
        for shift, (rows, columns) in enumerate(NEAR):
            row = lax.rem(y + (2 * SIDE - step + rows), SIDE)
            column = lax.rem(x + (3 * SIDE - 2 * step + columns), SIDE)
            at = (hop * SIDE + shift) * PAD
            for place in range(OWN):
                gathered[place, at : at + PAD, :] = s_ref[row * SIDE + column, place]
    for place in range(OWN):
        found = jnp.dot(p_ref[place], gathered[place], preferred_element_type=F32)
        for part in range(2):
            rows = pl.ds(2 * place + part, DEGREES, stride=2 * OWN)
            spread[rows, :] = found[:, part * CH : (part + 1) * CH]
    out_ref[...] = spread[...].astype(BF16)


def fourier_factors():
    rows = jnp.arange(2 * ORDERS, dtype=jnp.int32)[None, :]
    part = rows % (2 * HELD) // HELD
    order = rows // (2 * HELD) * HELD + rows % HELD
    device = jnp.arange(LON, dtype=jnp.int32)[:, None]
    within = jnp.arange(PAD, dtype=jnp.int32)[:, None]
    weight = jnp.where(order == 0, 1.0, 2.0).astype(F32) / jnp.sqrt(F32(NLON))
    weight = jnp.where(within < COLS, weight, 0.0)
    turn = 2.0 * jnp.pi / NLON
    first = (device * COLS * order % NLON).astype(F32) * turn
    rest = ((within * order + part * (NLON // 4)) % NLON).astype(F32) * turn
    return jnp.cos(first), jnp.sin(first), weight * jnp.cos(rest), weight * jnp.sin(rest)


def fourier_table(cos_a, sin_a, cos_b, sin_b, out_ref, tall):
    for d in range(LON):
        row = slice(d, d + 1)
        tall[d * PAD : (d + 1) * PAD, :] = (
            cos_a[row, :] * cos_b[...] - sin_a[row, :] * sin_b[...]
        )
    out_ref[...] = tall[...].T.astype(BF16)


def along(axis, value, step):
    return lax.ppermute(value, axis, [(i, (i + step) % SIDE) for i in range(SIDE)])


def same_colour(value, step):
    pairs = []
    for y in range(SIDE):
        for x in range(SIDE):
            to = (y + step) % SIDE * SIDE + (x + 2 * step) % SIDE
            pairs.append((y * SIDE + x, to))
    return lax.ppermute(value, ("y", "x"), pairs)


def on_device(grad_field, legendre):
    colour = (lax.axis_index("x") + 2 * lax.axis_index("y")) % SIDE
    struct = jax.ShapeDtypeStruct

    packed = call(
        pack_rows,
        struct((LON * SENT, CH), BF16),
        [pltpu.VMEM((PAD, CH), F32), pltpu.VMEM((LON * SENT, CH), F32)],
    )(grad_field)
    packed = packed.reshape(LON, SENT // 2, 2, CH)
    row_columns = lax.all_to_all(packed, "lon", 0, 0, tiled=True).reshape(LON * SENT, CH)

    masked = call(
        pack_legendre,
        struct((SIDE, TILES, PAD, CH), BF16),
        [pltpu.VMEM((PAD, (FULL + 1) * CH), F32)],
    )(legendre)
    line = [lax.dynamic_index_in_dim(masked, colour, 0, keepdims=False)]
    for rows, columns in NEAR[1:]:
        theirs = (colour - 2 * rows - columns) % SIDE
        theirs = lax.dynamic_index_in_dim(masked, theirs, 0, keepdims=False)
        line.append(along("y" if rows else "x", theirs, -rows - columns))
    line = jnp.stack(line)
    table = call(
        fourier_table,
        struct((2 * ORDERS, LON * PAD), BF16),
        [pltpu.VMEM((LON * PAD, 2 * ORDERS), F32)],
        n_in=4,
        vmem=16,
    )(*fourier_factors())
    line, table = lax.optimization_barrier((line, table))
    lines = [line] + [same_colour(line, step) for step in HOPS[1:]]
    upright = call(
        turn_legendre,
        struct((OWN, DEGREES, LAT * PAD), BF16),
        [pltpu.VMEM((LAT * PAD, CH), F32)],
        n_in=SIDE,
        cost=LONG,
    )(*lines)

    returned = call(
        spectrum_rows,
        struct((LON * BACK, CH), BF16),
        [
            pltpu.VMEM((LON * PAD, 2 * CH), BF16),
            pltpu.VMEM((LON * BACK, CH), F32),
            pltpu.VMEM((LON * SENT + 8, CH), F32),
            pltpu.VMEM((PAD, CH), F32),
        ],
        n_in=2,
    )(row_columns, table)
    returned = returned.reshape(LON, BACK // 2, 2, CH)
    by_sender = lax.all_to_all(returned, "lon", 0, 0, tiled=True).reshape(LON * BACK, CH)
    by_sender, upright = lax.optimization_barrier((by_sender, upright))
    turned = call(
        turn_rows,
        struct((LAT, OWN, PAD, 2 * CH), BF16),
        [pltpu.VMEM((LON * BACK, CH), F32)],
    )(by_sender)
    spectrum = lax.all_to_all(turned, ("y", "x"), 0, 0, tiled=True)

    middle = DEGREES * OWN
    own = call(
        legendre_sum,
        struct((2 * middle, CH), BF16),
        [
            pltpu.VMEM((OWN, LAT * PAD, 2 * CH), BF16),
            pltpu.VMEM((2 * middle, CH), F32),
        ],
        n_in=2,
    )(spectrum, upright)

    after = along("x", own, -1)
    before = along("x", own, 1)
    low = along("y", own[:middle], 1)
    high = along("y", own[middle:], -1)
    parts = [(own, 0, 0), (low, 2, 0), (high, 2, DEGREES // 2), (after, 1, 0), (before, 3, 0)]
    out = jnp.zeros((DEGREES, HELD, 2, CH), BF16)
    for value, step, start in parts:
        value = value.reshape(-1, OWN, 2, CH)
        at = (colour + step) % SIDE * OWN
        out = lax.dynamic_update_slice(out, value, (start, at, 0, 0))
    return out


def solution(mesh):
    fine = Mesh(mesh.devices.reshape(SIDE, SIDE, LON), ("y", "x", "lon"))
    return jax.shard_map(
        on_device,
        mesh=fine,
        in_specs=(P(("y", "x"), "lon", None), P("lon", ("y", "x"), None)),
        out_specs=P(None, "lon", None, None),
        check_vma=False,
    )
```

```python
import jax
import jax.numpy as jnp
from jax import lax
from jax.experimental import pallas as pl
from jax.experimental.pallas import tpu as pltpu
from jax.sharding import Mesh, PartitionSpec as P

DEGREES = 672
ORDERS = 384
NLON = 1440
CH = 128
SIDE = 4
LAT = SIDE * SIDE
LON = 32
ROWS = 45
COLS = 45
PAD = 48
HELD = ORDERS // LON
OWN = HELD // SIDE
EXTRA = ROWS - LON
HALF = (COLS + 1) // 2
SENT = COLS + HALF
LEAD = 40
BACK = 36
F32, BF16 = jnp.float32, jnp.bfloat16
HOPS = (0, 3, 1, 2)
NEAR = ((0, 0), (-1, 0), (0, -1), (0, 1))
MIB = 1024 * 1024
FULL = DEGREES // CH
TAIL = DEGREES % CH
TILES = OWN * FULL + 1

LONG = pl.CostEstimate(flops=10**11, transcendentals=0, bytes_accessed=10**9)


def call(body, out_shape, scratch=(), n_in=1, vmem=8, cost=None):
    whole = pl.BlockSpec(memory_space=pltpu.VMEM)
    many = isinstance(out_shape, list)
    return pl.pallas_call(
        body,
        out_shape=out_shape,
        in_specs=[whole] * n_in,
        out_specs=[whole] * len(out_shape) if many else whole,
        scratch_shapes=list(scratch),
        cost_estimate=cost,
        compiler_params=pltpu.CompilerParams(vmem_limit_bytes=vmem * MIB),
    )


def left_half(shape):
    return lax.broadcasted_iota(jnp.int32, shape, len(shape) - 1) < CH // 2


def pack_rows(grad_ref, out_ref, rows, flat):
    rows[...] = jnp.zeros_like(rows)
    left = left_half((HALF, CH))
    for d in range(2 * EXTRA, LON):
        flat[d * SENT + COLS : (d + 1) * SENT, :] = jnp.zeros((HALF, CH), F32)
    for row in range(ROWS):
        if row < LON:
            flat[row * SENT : row * SENT + COLS, :] = grad_ref[row].astype(F32)
        else:
            rows[0:COLS, :] = grad_ref[row].astype(F32)
            early, late = rows[0:HALF, :], rows[HALF : 2 * HALF, :]
            first = jnp.where(left, early, pltpu.roll(late, CH // 2, 1))
            second = jnp.where(left, pltpu.roll(early, CH // 2, 1), late)
            at = 2 * (row - LON) * SENT
            flat[at + COLS : at + SENT, :] = first
            flat[at + SENT + COLS : at + 2 * SENT, :] = second
    out_ref[...] = flat[...].astype(BF16)


def spectrum_rows(x_ref, table_ref, out_ref, both, flat, got, rows):
    got[...] = jnp.zeros_like(got)
    rows[...] = jnp.zeros_like(rows)
    half = PAD // 2
    left = left_half((half, CH))
    for d in range(LON):
        at = d * PAD
        both[at : at + PAD, 0:CH] = x_ref[d * SENT : d * SENT + PAD, :]
        got[0 : SENT - LEAD, :] = x_ref[d * SENT + LEAD : (d + 1) * SENT, :].astype(F32)
        packed = got[COLS - LEAD : COLS - LEAD + half, :]
        rows[0:half, :] = jnp.where(left, packed, 0.0)
        rows[HALF : HALF + half, :] = jnp.where(left, pltpu.roll(packed, CH // 2, 1), 0.0)
        both[at : at + PAD, CH : 2 * CH] = rows[...].astype(BF16)
    n = 2 * HELD
    found = jnp.dot(table_ref[...], both[...], preferred_element_type=F32)
    for d in range(LON):
        at = d * BACK
        flat[at : at + n, :] = found[d * n : (d + 1) * n, 0:CH]
        part = found[d * n : (d + 1) * n, CH : 2 * CH]
        high = pltpu.roll(part, CH // 2, 1)[HELD:n]
        flat[at + n : at + BACK, :] = jnp.where(left_half((HELD, CH)), part[0:HELD], high)
    out_ref[...] = flat[...].astype(BF16)


def turn_rows(r_ref, out_ref, flat):
    flat[...] = r_ref[...].astype(F32)
    n = 2 * HELD
    left = left_half((16, CH))
    for order in range(HELD):
        colour, place = divmod(order, OWN)
        for part in range(2):
            i = part * HELD + order
            lanes = slice(part * CH, (part + 1) * CH)
            main = flat[pl.ds(i, LON, stride=BACK), :]
            at = n + i % HELD
            even = flat[pl.ds(at, 16, stride=2 * BACK), :]
            odd = flat[pl.ds(BACK + at, 16, stride=2 * BACK), :]
            if part == 0:
                rest = jnp.where(left, even, pltpu.roll(odd, CH // 2, 1))
            else:
                rest = jnp.where(left, pltpu.roll(even, CH // 2, 1), odd)
            column = jnp.concatenate([main, rest], 0).astype(BF16)
            for t in range(LAT):
                if (t % SIDE + 2 * (t // SIDE)) % SIDE == colour:
                    out_ref[t, place, :, lanes] = column


def pack_legendre(legendre_ref, out_ref, wide):
    lon = lax.axis_index("lon")
    wide[...] = jnp.zeros_like(wide)
    degree = lax.broadcasted_iota(jnp.int32, (ROWS, DEGREES), 1)
    for colour in range(SIDE):
        tails = jnp.zeros((PAD, CH), F32)
        for place in range(OWN):
            order = colour * OWN + place
            value = legendre_ref[order].astype(F32)
            wide[0:ROWS, 0:DEGREES] = jnp.where(degree >= lon * HELD + order, value, 0.0)
            for tile in range(FULL):
                lanes = slice(tile * CH, (tile + 1) * CH)
                out_ref[colour, place * FULL + tile] = wide[:, lanes].astype(BF16)
            tail = wide[:, FULL * CH : (FULL + 1) * CH]
            tails += pltpu.roll(tail, place * TAIL, 1)
        out_ref[colour, TILES - 1] = tails.astype(BF16)


def turn_legendre(*refs):
    *parts, out_ref, tall = refs
    for tile in range(TILES):
        for hop, part in enumerate(parts):
            for shift in range(SIDE):
                at = (hop * SIDE + shift) * PAD
                tall[at : at + PAD, :] = part[shift, tile].astype(F32)
        turned = tall[...].T.astype(BF16)
        if tile == TILES - 1:
            for place in range(OWN):
                rows = slice(place * TAIL, (place + 1) * TAIL)
                out_ref[place, FULL * CH : DEGREES, :] = turned[rows]
        else:
            place, at = tile // FULL, tile % FULL * CH
            out_ref[place, at : at + CH, :] = turned


def legendre_sum(s_ref, p_ref, out_ref, gathered, spread):
    y, x = lax.axis_index("y"), lax.axis_index("x")
    for hop, step in enumerate(HOPS):
        for shift, (rows, columns) in enumerate(NEAR):
            row = lax.rem(y + (2 * SIDE - step + rows), SIDE)
            column = lax.rem(x + (3 * SIDE - 2 * step + columns), SIDE)
            at = (hop * SIDE + shift) * PAD
            for place in range(OWN):
                gathered[place, at : at + PAD, :] = s_ref[row * SIDE + column, place]
    for place in range(OWN):
        found = jnp.dot(p_ref[place], gathered[place], preferred_element_type=F32)
        for part in range(2):
            rows = pl.ds(2 * place + part, DEGREES, stride=2 * OWN)
            spread[rows, :] = found[:, part * CH : (part + 1) * CH]
    out_ref[...] = spread[...].astype(BF16)


def fourier_factors():
    rows = jnp.arange(2 * ORDERS, dtype=jnp.int32)[None, :]
    part = rows % (2 * HELD) // HELD
    order = rows // (2 * HELD) * HELD + rows % HELD
    device = jnp.arange(LON, dtype=jnp.int32)[:, None]
    within = jnp.arange(PAD, dtype=jnp.int32)[:, None]
    weight = jnp.where(order == 0, 1.0, 2.0).astype(F32) / jnp.sqrt(F32(NLON))
    weight = jnp.where(within < COLS, weight, 0.0)
    turn = 2.0 * jnp.pi / NLON
    first = (device * COLS * order % NLON).astype(F32) * turn
    rest = ((within * order + part * (NLON // 4)) % NLON).astype(F32) * turn
    return jnp.cos(first), jnp.sin(first), weight * jnp.cos(rest), weight * jnp.sin(rest)


def fourier_table(cos_a, sin_a, cos_b, sin_b, out_ref, tall):
    for d in range(LON):
        row = slice(d, d + 1)
        tall[d * PAD : (d + 1) * PAD, :] = (
            cos_a[row, :] * cos_b[...] - sin_a[row, :] * sin_b[...]
        )
    out_ref[...] = tall[...].T.astype(BF16)


def along(axis, value, step):
    return lax.ppermute(value, axis, [(i, (i + step) % SIDE) for i in range(SIDE)])


def same_colour(value, step):
    pairs = []
    for y in range(SIDE):
        for x in range(SIDE):
            to = (y + step) % SIDE * SIDE + (x + 2 * step) % SIDE
            pairs.append((y * SIDE + x, to))
    return lax.ppermute(value, ("y", "x"), pairs)


def on_device(grad_field, legendre):
    colour = (lax.axis_index("x") + 2 * lax.axis_index("y")) % SIDE
    struct = jax.ShapeDtypeStruct

    packed = call(
        pack_rows,
        struct((LON * SENT, CH), BF16),
        [pltpu.VMEM((PAD, CH), F32), pltpu.VMEM((LON * SENT, CH), F32)],
    )(grad_field)
    packed = packed.reshape(LON, SENT // 2, 2, CH)
    row_columns = lax.all_to_all(packed, "lon", 0, 0, tiled=True).reshape(LON * SENT, CH)

    masked = call(
        pack_legendre,
        struct((SIDE, TILES, PAD, CH), BF16),
        [pltpu.VMEM((PAD, (FULL + 1) * CH), F32)],
    )(legendre)
    line = [lax.dynamic_index_in_dim(masked, colour, 0, keepdims=False)]
    for rows, columns in NEAR[1:]:
        theirs = (colour - 2 * rows - columns) % SIDE
        theirs = lax.dynamic_index_in_dim(masked, theirs, 0, keepdims=False)
        line.append(along("y" if rows else "x", theirs, -rows - columns))
    line = jnp.stack(line)
    table = call(
        fourier_table,
        struct((2 * ORDERS, LON * PAD), BF16),
        [pltpu.VMEM((LON * PAD, 2 * ORDERS), F32)],
        n_in=4,
        vmem=16,
    )(*fourier_factors())
    line, table = lax.optimization_barrier((line, table))
    lines = [line] + [same_colour(line, step) for step in HOPS[1:]]
    upright = call(
        turn_legendre,
        struct((OWN, DEGREES, LAT * PAD), BF16),
        [pltpu.VMEM((LAT * PAD, CH), F32)],
        n_in=SIDE,
        cost=LONG,
    )(*lines)

    returned = call(
        spectrum_rows,
        struct((LON * BACK, CH), BF16),
        [
            pltpu.VMEM((LON * PAD, 2 * CH), BF16),
            pltpu.VMEM((LON * BACK, CH), F32),
            pltpu.VMEM((PAD, CH), F32),
            pltpu.VMEM((PAD, CH), F32),
        ],
        n_in=2,
    )(row_columns, table)
    returned = returned.reshape(LON, BACK // 2, 2, CH)
    by_sender = lax.all_to_all(returned, "lon", 0, 0, tiled=True).reshape(LON * BACK, CH)
    by_sender, upright = lax.optimization_barrier((by_sender, upright))
    turned = call(
        turn_rows,
        struct((LAT, OWN, PAD, 2 * CH), BF16),
        [pltpu.VMEM((LON * BACK, CH), F32)],
    )(by_sender)
    spectrum = lax.all_to_all(turned, ("y", "x"), 0, 0, tiled=True)

    middle = DEGREES * OWN
    own = call(
        legendre_sum,
        struct((2 * middle, CH), BF16),
        [
            pltpu.VMEM((OWN, LAT * PAD, 2 * CH), BF16),
            pltpu.VMEM((2 * middle, CH), F32),
        ],
        n_in=2,
    )(spectrum, upright)

    after = along("x", own, -1)
    before = along("x", own, 1)
    low = along("y", own[:middle], 1)
    high = along("y", own[middle:], -1)
    parts = [(own, 0, 0), (low, 2, 0), (high, 2, DEGREES // 2), (after, 1, 0), (before, 3, 0)]
    out = jnp.zeros((DEGREES, HELD, 2, CH), BF16)
    for value, step, start in parts:
        value = value.reshape(-1, OWN, 2, CH)
        at = (colour + step) % SIDE * OWN
        out = lax.dynamic_update_slice(out, value, (start, at, 0, 0))
    return out


def solution(mesh):
    fine = Mesh(mesh.devices.reshape(SIDE, SIDE, LON), ("y", "x", "lon"))
    return jax.shard_map(
        on_device,
        mesh=fine,
        in_specs=(P(("y", "x"), "lon", None), P("lon", ("y", "x"), None)),
        out_specs=P(None, "lon", None, None),
        check_vma=False,
    )
```

```python
import jax
import jax.numpy as jnp
from jax import lax
from jax.experimental import pallas as pl
from jax.experimental.pallas import tpu as pltpu
from jax.sharding import Mesh, PartitionSpec as P

DEGREES = 672
ORDERS = 384
NLON = 1440
CH = 128
SIDE = 4
LAT = SIDE * SIDE
LON = 32
ROWS = 45
COLS = 45
PAD = 48
HELD = ORDERS // LON
OWN = HELD // SIDE
EXTRA = ROWS - LON
HALF = (COLS + 1) // 2
SENT = COLS + HALF
LEAD = 40
BACK = 36
F32, BF16 = jnp.float32, jnp.bfloat16
HOPS = (0, 3, 1, 2)
NEAR = ((0, 0), (-1, 0), (0, -1), (0, 1))
MIB = 1024 * 1024
FULL = DEGREES // CH
TAIL = DEGREES % CH
TILES = OWN * FULL + 1

LONG = pl.CostEstimate(flops=10**11, transcendentals=0, bytes_accessed=10**9)


def call(body, out_shape, scratch=(), n_in=1, vmem=8, cost=None):
    whole = pl.BlockSpec(memory_space=pltpu.VMEM)
    many = isinstance(out_shape, list)
    return pl.pallas_call(
        body,
        out_shape=out_shape,
        in_specs=[whole] * n_in,
        out_specs=[whole] * len(out_shape) if many else whole,
        scratch_shapes=list(scratch),
        cost_estimate=cost,
        compiler_params=pltpu.CompilerParams(vmem_limit_bytes=vmem * MIB),
    )


def left_half(shape):
    return lax.broadcasted_iota(jnp.int32, shape, len(shape) - 1) < CH // 2


def pack_rows(grad_ref, out_ref, rows, flat):
    rows[...] = jnp.zeros_like(rows)
    left = left_half((HALF, CH))
    for d in range(2 * EXTRA, LON):
        flat[d * SENT + COLS : (d + 1) * SENT, :] = jnp.zeros((HALF, CH), F32)
    for row in range(ROWS):
        if row < LON:
            flat[row * SENT : row * SENT + COLS, :] = grad_ref[row].astype(F32)
        else:
            rows[0:COLS, :] = grad_ref[row].astype(F32)
            early, late = rows[0:HALF, :], rows[HALF : 2 * HALF, :]
            first = jnp.where(left, early, pltpu.roll(late, CH // 2, 1))
            second = jnp.where(left, pltpu.roll(early, CH // 2, 1), late)
            at = 2 * (row - LON) * SENT
            flat[at + COLS : at + SENT, :] = first
            flat[at + SENT + COLS : at + 2 * SENT, :] = second
    out_ref[...] = flat[...].astype(BF16)


def spectrum_rows(x_ref, table_ref, out_ref, both, flat, got, rows):
    got[...] = jnp.zeros_like(got)
    rows[...] = jnp.zeros_like(rows)
    half = PAD // 2
    left = left_half((half, CH))
    for d in range(LON):
        at = d * PAD
        both[at : at + PAD, 0:CH] = x_ref[d * SENT : d * SENT + PAD, :]
        got[0 : SENT - LEAD, :] = x_ref[d * SENT + LEAD : (d + 1) * SENT, :].astype(F32)
        packed = got[COLS - LEAD : COLS - LEAD + half, :]
        rows[0:half, :] = jnp.where(left, packed, 0.0)
        rows[HALF : HALF + half, :] = jnp.where(left, pltpu.roll(packed, CH // 2, 1), 0.0)
        both[at : at + PAD, CH : 2 * CH] = rows[...].astype(BF16)
    n = 2 * HELD
    found = jnp.dot(table_ref[...], both[...], preferred_element_type=F32)
    for d in range(LON):
        at = d * BACK
        flat[at : at + n, :] = found[d * n : (d + 1) * n, 0:CH]
        part = found[d * n : (d + 1) * n, CH : 2 * CH]
        high = pltpu.roll(part, CH // 2, 1)[HELD:n]
        flat[at + n : at + BACK, :] = jnp.where(left_half((HELD, CH)), part[0:HELD], high)
    out_ref[...] = flat[...].astype(BF16)


def turn_rows(r_ref, out_ref, flat):
    flat[...] = r_ref[...].astype(F32)
    n = 2 * HELD
    left = left_half((16, CH))
    for order in range(HELD):
        colour, place = divmod(order, OWN)
        for part in range(2):
            i = part * HELD + order
            lanes = slice(part * CH, (part + 1) * CH)
            main = flat[pl.ds(i, LON, stride=BACK), :]
            at = n + i % HELD
            even = flat[pl.ds(at, 16, stride=2 * BACK), :]
            odd = flat[pl.ds(BACK + at, 16, stride=2 * BACK), :]
            if part == 0:
                rest = jnp.where(left, even, pltpu.roll(odd, CH // 2, 1))
            else:
                rest = jnp.where(left, pltpu.roll(even, CH // 2, 1), odd)
            column = jnp.concatenate([main, rest], 0).astype(BF16)
            for t in range(LAT):
                if (t % SIDE + 2 * (t // SIDE)) % SIDE == colour:
                    out_ref[t, place, :, lanes] = column


def pack_legendre(legendre_ref, out_ref, wide):
    lon = lax.axis_index("lon")
    wide[...] = jnp.zeros_like(wide)
    degree = lax.broadcasted_iota(jnp.int32, (ROWS, DEGREES), 1)
    for colour in range(SIDE):
        tails = jnp.zeros((PAD, CH), F32)
        for place in range(OWN):
            order = colour * OWN + place
            value = legendre_ref[order].astype(F32)
            wide[0:ROWS, 0:DEGREES] = jnp.where(degree >= lon * HELD + order, value, 0.0)
            for tile in range(FULL):
                lanes = slice(tile * CH, (tile + 1) * CH)
                out_ref[colour, place * FULL + tile] = wide[:, lanes].astype(BF16)
            tail = wide[:, FULL * CH : (FULL + 1) * CH]
            tails += pltpu.roll(tail, place * TAIL, 1)
        out_ref[colour, TILES - 1] = tails.astype(BF16)


def turn_legendre(*refs):
    *parts, out_ref, turned, tall, done = refs
    copies = [
        pltpu.make_async_copy(turned.at[place], out_ref.at[place], done.at[place])
        for place in range(OWN)
    ]
    for tile in [TILES - 1] + list(range(TILES - 1)):
        for hop, part in enumerate(parts):
            for shift in range(SIDE):
                at = (hop * SIDE + shift) * PAD
                tall[at : at + PAD, :] = part[shift, tile].astype(F32)
        found = tall[...].T.astype(BF16)
        if tile == TILES - 1:
            for place in range(OWN):
                rows = slice(place * TAIL, (place + 1) * TAIL)
                turned[place, FULL * CH : DEGREES, :] = found[rows]
        else:
            place, at = tile // FULL, tile % FULL * CH
            turned[place, at : at + CH, :] = found
            if tile % FULL == FULL - 1:
                copies[place].start()
    for copy in copies:
        copy.wait()


def legendre_sum(s_ref, p_ref, out_ref, gathered, spread):
    y, x = lax.axis_index("y"), lax.axis_index("x")
    for hop, step in enumerate(HOPS):
        for shift, (rows, columns) in enumerate(NEAR):
            row = lax.rem(y + (2 * SIDE - step + rows), SIDE)
            column = lax.rem(x + (3 * SIDE - 2 * step + columns), SIDE)
            at = (hop * SIDE + shift) * PAD
            for place in range(OWN):
                gathered[place, at : at + PAD, :] = s_ref[row * SIDE + column, place]
    for place in range(OWN):
        found = jnp.dot(p_ref[place], gathered[place], preferred_element_type=F32)
        for part in range(2):
            rows = pl.ds(2 * place + part, DEGREES, stride=2 * OWN)
            spread[rows, :] = found[:, part * CH : (part + 1) * CH]
    out_ref[...] = spread[...].astype(BF16)


def fourier_factors():
    rows = jnp.arange(2 * ORDERS, dtype=jnp.int32)[None, :]
    part = rows % (2 * HELD) // HELD
    order = rows // (2 * HELD) * HELD + rows % HELD
    device = jnp.arange(LON, dtype=jnp.int32)[:, None]
    within = jnp.arange(PAD, dtype=jnp.int32)[:, None]
    weight = jnp.where(order == 0, 1.0, 2.0).astype(F32) / jnp.sqrt(F32(NLON))
    weight = jnp.where(within < COLS, weight, 0.0)
    turn = 2.0 * jnp.pi / NLON
    first = (device * COLS * order % NLON).astype(F32) * turn
    rest = ((within * order + part * (NLON // 4)) % NLON).astype(F32) * turn
    return jnp.cos(first), jnp.sin(first), weight * jnp.cos(rest), weight * jnp.sin(rest)


def fourier_table(cos_a, sin_a, cos_b, sin_b, out_ref, tall):
    for d in range(LON):
        row = slice(d, d + 1)
        tall[d * PAD : (d + 1) * PAD, :] = (
            cos_a[row, :] * cos_b[...] - sin_a[row, :] * sin_b[...]
        )
    out_ref[...] = tall[...].T.astype(BF16)


def along(axis, value, step):
    return lax.ppermute(value, axis, [(i, (i + step) % SIDE) for i in range(SIDE)])


def same_colour(value, step):
    pairs = []
    for y in range(SIDE):
        for x in range(SIDE):
            to = (y + step) % SIDE * SIDE + (x + 2 * step) % SIDE
            pairs.append((y * SIDE + x, to))
    return lax.ppermute(value, ("y", "x"), pairs)


def on_device(grad_field, legendre):
    colour = (lax.axis_index("x") + 2 * lax.axis_index("y")) % SIDE
    struct = jax.ShapeDtypeStruct

    packed = call(
        pack_rows,
        struct((LON * SENT, CH), BF16),
        [pltpu.VMEM((PAD, CH), F32), pltpu.VMEM((LON * SENT, CH), F32)],
    )(grad_field)
    packed = packed.reshape(LON, SENT // 2, 2, CH)
    row_columns = lax.all_to_all(packed, "lon", 0, 0, tiled=True).reshape(LON * SENT, CH)

    masked = call(
        pack_legendre,
        struct((SIDE, TILES, PAD, CH), BF16),
        [pltpu.VMEM((PAD, (FULL + 1) * CH), F32)],
    )(legendre)
    line = [lax.dynamic_index_in_dim(masked, colour, 0, keepdims=False)]
    for rows, columns in NEAR[1:]:
        theirs = (colour - 2 * rows - columns) % SIDE
        theirs = lax.dynamic_index_in_dim(masked, theirs, 0, keepdims=False)
        line.append(along("y" if rows else "x", theirs, -rows - columns))
    line = jnp.stack(line)
    table = call(
        fourier_table,
        struct((2 * ORDERS, LON * PAD), BF16),
        [pltpu.VMEM((LON * PAD, 2 * ORDERS), F32)],
        n_in=4,
        vmem=16,
    )(*fourier_factors())
    line, table = lax.optimization_barrier((line, table))
    lines = [line] + [same_colour(line, step) for step in HOPS[1:]]
    whole = pl.BlockSpec(memory_space=pltpu.VMEM)
    upright = pl.pallas_call(
        turn_legendre,
        out_shape=struct((OWN, DEGREES, LAT * PAD), BF16),
        in_specs=[whole] * SIDE,
        out_specs=pl.BlockSpec(memory_space=pltpu.HBM),
        scratch_shapes=[
            pltpu.VMEM((OWN, DEGREES, LAT * PAD), BF16),
            pltpu.VMEM((LAT * PAD, CH), F32),
            pltpu.SemaphoreType.DMA((OWN,)),
        ],
        cost_estimate=LONG,
        compiler_params=pltpu.CompilerParams(vmem_limit_bytes=12 * MIB),
    )(*lines)

    returned = call(
        spectrum_rows,
        struct((LON * BACK, CH), BF16),
        [
            pltpu.VMEM((LON * PAD, 2 * CH), BF16),
            pltpu.VMEM((LON * BACK, CH), F32),
            pltpu.VMEM((PAD, CH), F32),
            pltpu.VMEM((PAD, CH), F32),
        ],
        n_in=2,
    )(row_columns, table)
    returned = returned.reshape(LON, BACK // 2, 2, CH)
    by_sender = lax.all_to_all(returned, "lon", 0, 0, tiled=True).reshape(LON * BACK, CH)
    by_sender, upright = lax.optimization_barrier((by_sender, upright))
    turned = call(
        turn_rows,
        struct((LAT, OWN, PAD, 2 * CH), BF16),
        [pltpu.VMEM((LON * BACK, CH), F32)],
    )(by_sender)
    spectrum = lax.all_to_all(turned, ("y", "x"), 0, 0, tiled=True)

    middle = DEGREES * OWN
    own = call(
        legendre_sum,
        struct((2 * middle, CH), BF16),
        [
            pltpu.VMEM((OWN, LAT * PAD, 2 * CH), BF16),
            pltpu.VMEM((2 * middle, CH), F32),
        ],
        n_in=2,
    )(spectrum, upright)

    after = along("x", own, -1)
    before = along("x", own, 1)
    low = along("y", own[:middle], 1)
    high = along("y", own[middle:], -1)
    parts = [(own, 0, 0), (low, 2, 0), (high, 2, DEGREES // 2), (after, 1, 0), (before, 3, 0)]
    out = jnp.zeros((DEGREES, HELD, 2, CH), BF16)
    for value, step, start in parts:
        value = value.reshape(-1, OWN, 2, CH)
        at = (colour + step) % SIDE * OWN
        out = lax.dynamic_update_slice(out, value, (start, at, 0, 0))
    return out


def solution(mesh):
    fine = Mesh(mesh.devices.reshape(SIDE, SIDE, LON), ("y", "x", "lon"))
    return jax.shard_map(
        on_device,
        mesh=fine,
        in_specs=(P(("y", "x"), "lon", None), P("lon", ("y", "x"), None)),
        out_specs=P(None, "lon", None, None),
        check_vma=False,
    )
```
